32 devices in a mesh: row: 4 (over z), col: 8 (over y, x, core).
Axes of the slice: x: 2, y: 2, z: 4, core: 2. Of those that a mesh axis runs over, the one named last changes fastest.
Arguments:
- field: float32 [32, 196608], P(None, ('row', 'col')), may hold values from -6 to 6
- incident: float32 [32, 98304], P(None, 'col'), may hold values from -6 to 6
- elem_mat: float32 [4, 4, 1179648], P(None, None, ('row', 'col')), may hold values from -1.5 to 1.5
- connect: int32 [4, 1179648], P(None, ('row', 'col')), may hold values from 0 to 9215
- halo_lists: int32 [32, 2, 1536], P(('row', 'col')), may hold values from 0 to 6143
- bem_rows: float32 [256, 98304], P('row', 'col'), may hold values from -0.01953125 to 0.01953125
- send_node: int32 [32, 8, 768], P(('row', 'col')), may hold values from 0 to 6143, as said below
- send_count: int32 [32, 8], P(('row', 'col')), may hold values from 0 to 768, as said below
- block_slots: int32 [8, 32, 768], P('col'), may hold values from 0 to 12287, as said below
Outputs:
- fem_out: float32 [32, 196608], P(None, ('row', 'col'))
- bem_out: float32 [32, 256], P(None, 'row')
The draws below stay inside these ranges and needn't reach their ends.
Inputs may be any that keep to these rules, and one draw needn't show every extreme that they name: `send_count`: each column block's 12288 positions are split among the partitions' live slots; in every block some partition fills all 768 slots. `send_node`: live slots of one partition name distinct own nodes; slots at or beyond the count hold 0. `block_slots`: the live slots of all partitions cover each position of block c exactly once; slots at or beyond the count hold 0.
All inputs are finite; a program needn't handle non-finite values.
Results may differ from the reference program's by a relative error of at most 0.0003.
Values sent between devices are 32-bit elements; how exact they have to be, the bound alone decides.
A program may use at most 256 MiB of HBM per device.

```python
import jax
import jax.numpy as jnp
from jax import lax

S = 32
NB = 98304
NODE_DEV = 6144
BLOCKS = 8
BLK = 12288
OWNERS = 32
SLAB = 256
HALO = 1536
ELEM_DEV = 36864
NODES = 196608
ELEMS = 1179648
CAP = 768


def trace_tables(key):
    mean_load = NB // (OWNERS * BLOCKS)
    base = jax.random.fold_in(key, 7)
    keys = jax.random.split(base, 5)
    pairs = OWNERS // 2
    leaning = jax.random.randint(keys[0], (pairs, 1), -mean_load, mean_load + 1)
    jitter = jax.random.randint(keys[1], (pairs, BLOCKS), -(mean_load // 4), mean_load // 4 + 1)
    offset_load = jnp.clip(leaning + jitter, -mean_load, mean_load)
    heavy = jax.random.randint(keys[2], (1, BLOCKS), 0, pairs)
    offset_load = jnp.where(jnp.arange(pairs)[:, None] == heavy, mean_load, offset_load)
    counts = jnp.stack([mean_load + offset_load, mean_load - offset_load], axis=1).reshape(OWNERS, BLOCKS).astype(jnp.int32)
    slot_range = jnp.arange(CAP, dtype=jnp.int32)
    live_slots = slot_range[None, None, :] < counts[:, :, None]

    def block_order(sub):
        return jax.random.permutation(sub, BLK)

    def node_order(sub):
        return jax.random.permutation(sub, NODE_DEV)
    block_perm = jax.vmap(block_order)(jax.random.split(keys[3], BLOCKS))
    start_block = jnp.cumsum(counts, axis=0) - counts
    where_block = jnp.minimum(start_block[:, :, None] + slot_range, BLK - 1)
    positions = block_perm[jnp.arange(BLOCKS)[None, :, None], where_block]
    positions = jnp.where(live_slots, positions, 0).astype(jnp.int32)
    node_perm = jax.vmap(node_order)(jax.random.split(keys[4], OWNERS))
    start_owner = jnp.cumsum(counts, axis=1) - counts
    where_node = jnp.minimum(start_owner[:, :, None] + slot_range, NODE_DEV - 1)
    nodes = node_perm[jnp.arange(OWNERS)[:, None, None], where_node]
    nodes = jnp.where(live_slots, nodes, 0).astype(jnp.int32)
    return (nodes, counts, jnp.transpose(positions, (1, 0, 2)))


def draw_send_node(key, part):
    return trace_tables(key)[0]


def draw_send_count(key, part):
    return trace_tables(key)[1]


def draw_block_slots(key, part):
    return trace_tables(key)[2]


def plant(array, rng, least, top_value):
    extent = array.shape
    place = [jax.random.randint(jax.random.fold_in(rng, axis), (), 0, extent[axis]) for axis in range(len(extent))]
    array = array.at[tuple(place)].set(least)
    longest = extent.index(max(extent))
    place[longest] = (place[longest] + 1) % extent[longest]
    return array.at[tuple(place)].set(top_value)


def shard_levels(own_key, extent, cuts, smallest, top_value):
    loudness, own = 1.0, jax.random.fold_in(own_key, 6)
    for dim, parts in cuts:
        heights = jnp.exp(jax.random.uniform(jax.random.fold_in(own, dim), (parts,), jnp.float32, smallest / len(cuts), top_value / len(cuts)))
        loudness = loudness * jnp.repeat(heights, extent[dim] // parts).reshape([-1 if axis == dim else 1 for axis in range(len(extent))])
    return loudness


def normal_values(key, dims, spread, reach, shards=(), kind=jnp.bfloat16):
    drawn = spread * jax.random.normal(key, dims, jnp.float32)
    if shards:
        drawn = drawn * shard_levels(key, dims, shards, -0.22, 0.18)
    return jnp.clip(drawn, -reach, reach).astype(kind)


def setup_inputs(seed: int = 0) -> dict:
    seeds = jax.random.split(jax.random.key(seed), 10)
    field = normal_values(seeds[0], (S, NODES), 1.0, 6.0, ((1, 32),), jnp.float32)
    incident = normal_values(seeds[1], (S, NB), 1.0, 6.0, ((1, 8),), jnp.float32)
    elem_mat = normal_values(seeds[2], (4, 4, ELEMS), 0.25, 1.5, ((2, 32),), jnp.float32)
    connect = plant(jax.random.randint(seeds[3], (4, ELEMS), 0, NODE_DEV + 2 * HALO), jax.random.fold_in(seeds[3], 1), 0, (NODE_DEV + 2 * HALO) - 1).astype(jnp.int32)
    halo_lists = plant(jax.random.randint(seeds[4], (OWNERS, 2, HALO), 0, NODE_DEV), jax.random.fold_in(seeds[4], 1), 0, NODE_DEV - 1).astype(jnp.int32)
    bem_rows = normal_values(seeds[5], (SLAB, NB), NB ** -0.5, 0.01953125, ((0, 4), (1, 8)), jnp.float32)
    send_node = draw_send_node(jax.random.fold_in(seeds[9], 71), 0)
    send_count = draw_send_count(jax.random.fold_in(seeds[9], 71), 0)
    block_slots = draw_block_slots(jax.random.fold_in(seeds[9], 71), 0)
    return {"field": field, "incident": incident, "elem_mat": elem_mat, "connect": connect, "halo_lists": halo_lists, "bem_rows": bem_rows, "send_node": send_node, "send_count": send_count, "block_slots": block_slots}


def element_apply(extended, conn, mats, node_count, halo):
    gathered = extended[:, conn]
    terms = []
    for a in range(4):
        accum = mats[a, 0][None, :] * gathered[:, 0]
        for b in range(1, 4):
            accum = accum + mats[a, b][None, :] * gathered[:, b]
        terms.append(accum)
    element_terms = jnp.stack(terms, axis=1)
    owned_rows = conn - halo
    inside = (owned_rows >= 0) & (owned_rows < node_count)
    target = jnp.where(inside, owned_rows, node_count).astype(jnp.int32)
    result = jnp.zeros((extended.shape[0], node_count), jnp.float32)
    return result.at[:, target.reshape(-1)].add(element_terms.reshape(extended.shape[0], -1), mode="drop")


def reference(field, incident, elem_mat, connect, halo_lists, bem_rows, send_node, send_count, block_slots):
    field_blocks = jnp.transpose(field.reshape(S, OWNERS, NODE_DEV), (1, 0, 2))

    def pick_halo(block, lists):
        return block[:, lists.reshape(-1)].reshape(S, 2, HALO)

    outbound = jax.vmap(pick_halo)(field_blocks, halo_lists)
    empty = jnp.zeros((1, S, HALO), jnp.float32)
    from_prev = jnp.concatenate([empty, outbound[:-1, :, 1, :]], axis=0)
    from_next = jnp.concatenate([outbound[1:, :, 0, :], empty], axis=0)
    conn_blocks = jnp.transpose(connect.reshape(4, OWNERS, ELEM_DEV), (1, 0, 2))
    mat_blocks = jnp.transpose(elem_mat.reshape(4, 4, OWNERS, ELEM_DEV), (2, 0, 1, 3))

    def apply_part(items):
        block, prev_part, next_part, conn, mats = items
        extended = jnp.concatenate([prev_part, block, next_part], axis=1)
        return element_apply(extended, conn, mats, NODE_DEV, HALO)

    fem_blocks = lax.map(apply_part, (field_blocks, from_prev, from_next, conn_blocks, mat_blocks))
    fem_out = jnp.transpose(fem_blocks, (1, 0, 2)).reshape(S, OWNERS * NODE_DEV)

    def pick_trace(block, nodes, counts):
        picked = block[:, nodes.reshape(-1)].reshape(S, BLOCKS, CAP)
        live_slots = jnp.arange(CAP, dtype=jnp.int32)[None, :] < counts[:, None]
        return jnp.where(live_slots[None], picked, jnp.zeros_like(picked))

    traces = jax.vmap(pick_trace)(field_blocks, send_node, send_count)
    columns = jnp.transpose(block_slots, (1, 0, 2)) + (jnp.arange(BLOCKS, dtype=jnp.int32) * BLK)[None, :, None]
    surface = incident.at[:, columns.reshape(-1).astype(jnp.int32)].add(jnp.transpose(traces, (1, 0, 2, 3)).reshape(S, -1))
    bem_out = lax.dot_general(surface, bem_rows, (((1,), (1,)), ((), ())), precision=lax.Precision.HIGHEST, preferred_element_type=jnp.float32)
    return fem_out, bem_out
```

```python
import functools

import jax
import jax.numpy as jnp
from jax import lax
from jax.experimental import pallas as pl
from jax.experimental.pallas import tpu as pltpu
from jax.sharding import PartitionSpec as P

S = 32
LANES = 128
GROUP = 4 * LANES
SETS = 2
UNROLL = 64
VMEM_BYTES = 60 * 2**20


def lane_iota():
    return lax.broadcasted_iota(jnp.int32, (1, LANES), 1)


def quarter(parts):
    lane = lane_iota()
    low = jnp.where(lane < S, parts[0], parts[1])
    high = jnp.where(lane < 3 * S, parts[2], parts[3])
    return jnp.where(lane < 2 * S, low, high)


def aligned(start, size=LANES):
    return pl.ds(pl.multiple_of(start, LANES), size)


def fill_table(table, first, source):
    def step(i, carry):
        block = source[:, aligned(i * LANES)]
        table[aligned(first + i * LANES), :] = jnp.concatenate([block] * 4, axis=0).T
        return carry

    lax.fori_loop(0, source.shape[1] // LANES, step, 0)


def gather_rows(table, index, base, rows):
    def step(j, carry):
        start = pl.multiple_of(j * UNROLL, UNROLL)
        for u in range(UNROLL):
            picked = [
                table[pl.ds(index[base + b * LANES + start + u], 1), :] for b in range(4)
            ]
            rows[pl.ds(start + u, 1), :] = quarter(picked)
        return carry

    lax.fori_loop(0, LANES // UNROLL, step, 0)


def pick_kernel(index, field, out, table, rows):
    fill_table(table, 0, field)

    def group(k, carry):
        gather_rows(table, index, k * GROUP, rows)
        turned = rows[...].T
        for b in range(4):
            out[:, aligned(k * GROUP + b * LANES)] = turned[S * b : S * b + S]
        return carry

    lax.fori_loop(0, out.shape[1] // GROUP, group, 0)


def pick(index, field):
    return pl.pallas_call(
        pick_kernel,
        in_specs=[
            pl.BlockSpec(memory_space=pltpu.SMEM),
            pl.BlockSpec(memory_space=pltpu.VMEM),
        ],
        out_specs=pl.BlockSpec(memory_space=pltpu.VMEM),
        out_shape=jax.ShapeDtypeStruct((S, index.shape[0]), jnp.float32),
        scratch_shapes=[
            pltpu.VMEM((field.shape[1], LANES), jnp.float32),
            pltpu.VMEM((LANES, LANES), jnp.float32),
        ],
        compiler_params=pltpu.CompilerParams(vmem_limit_bytes=VMEM_BYTES),
        name="pick",
    )(index, field)


def element_kernel(halo, index, mats, low, field, high, out, table, rows, terms, *sums):
    step = pl.program_id(0)
    nodes = field.shape[1]

    @pl.when(step == 0)
    def _():
        fill_table(table, 0, low)
        fill_table(table, halo, field)
        fill_table(table, halo + nodes, high)

        def clear(i, carry):
            for total in sums:
                total[aligned(i * LANES), :] = jnp.zeros((LANES, LANES), jnp.float32)
            return carry

        lax.fori_loop(0, table.shape[0] // LANES, clear, 0)

    def block(k, carry):
        base = k * GROUP
        gather_rows(table, index, base, rows)
        turned = rows[...].T
        here = aligned(k * LANES)
        parts = []
        for a in range(4):
            part = mats[a, 0:1, here] * turned[0:S]
            for b in range(1, 4):
                part = part + mats[a, b : b + 1, here] * turned[S * b : S * b + S]
            parts.append(part)
        terms[...] = jnp.concatenate(parts, axis=0).T

        def scatter(j, inner):
            start = pl.multiple_of(j * UNROLL, UNROLL)
            for u in range(0, UNROLL, SETS):
                places, values = [], []
                for p in range(SETS):
                    term = terms[pl.ds(start + u + p, 1), :]
                    for a in range(4):
                        place = pl.ds(index[base + a * LANES + start + u + p], 1)
                        places.append(place)
                        values.append(sums[4 * p + a][place, :] + term)
                for total, place, value in zip(sums, places, values):
                    total[place, :] = value
            return inner

        lax.fori_loop(0, LANES // UNROLL, scatter, 0)
        return carry

    lax.fori_loop(0, mats.shape[2] // LANES, block, 0)

    @pl.when(step == pl.num_programs(0) - 1)
    def _():
        def finish(i, carry):
            here = aligned(i * LANES + halo)
            added = [
                sum(sums[4 * p + a][here, :] for p in range(1, SETS)) + sums[a][here, :]
                for a in range(4)
            ]
            turned = quarter(added).T
            out[:, aligned(i * LANES)] = (
                turned[0:S] + turned[S : 2 * S] + turned[2 * S : 3 * S] + turned[3 * S :]
            )
            return carry

        lax.fori_loop(0, nodes // LANES, finish, 0)


def element_apply(index, mats, low, field, high):
    halo, nodes = low.shape[1], field.shape[1]
    elements = mats.shape[2]
    blocks = next(n for n in (16, 12, 8, 4, 2) if elements % (n * LANES) == 0)
    table = pltpu.VMEM((nodes + 2 * halo, LANES), jnp.float32)
    square = pltpu.VMEM((LANES, LANES), jnp.float32)
    whole = pl.BlockSpec(memory_space=pltpu.VMEM)
    return pl.pallas_call(
        functools.partial(element_kernel, halo),
        grid=(elements // (blocks * LANES),),
        in_specs=[
            pl.BlockSpec((blocks * GROUP,), lambda i: (i,), memory_space=pltpu.SMEM),
            pl.BlockSpec((4, 4, blocks * LANES), lambda i: (0, 0, i)),
            whole,
            whole,
            whole,
        ],
        out_specs=whole,
        out_shape=jax.ShapeDtypeStruct((S, nodes), jnp.float32),
        scratch_shapes=[table, square, square] + [table] * (4 * SETS),
        compiler_params=pltpu.CompilerParams(vmem_limit_bytes=VMEM_BYTES),
        name="elements",
    )(index, mats, low, field, high)


def surface_kernel(index, values, incident, bem, out, surface, *rows):
    lane = lane_iota()

    def group(k, carry):
        stacked = jnp.concatenate(
            [values[:, aligned(k * GROUP + q * LANES)] for q in range(4)], axis=0
        )
        turned = stacked.T
        for q in range(4):
            rows[q][...] = jnp.where(
                (lane >= S * q) & (lane < S * q + S), turned, jnp.zeros_like(turned)
            )

        def scatter(j, inner):
            start = pl.multiple_of(j * UNROLL, UNROLL)
            for u in range(UNROLL):
                for q in range(4):
                    place = index[k * GROUP + q * LANES + start + u]
                    surface[pl.ds(place, 1), :] = rows[q][pl.ds(start + u, 1), :]
            return inner

        lax.fori_loop(0, LANES // UNROLL, scatter, 0)
        return carry

    lax.fori_loop(0, values.shape[1] // GROUP, group, 0)
    surface[0:1, :] = jnp.zeros((1, LANES), jnp.float32)
    spread = jnp.dot(
        bem[...],
        surface[...],
        precision=lax.Precision.HIGHEST,
        preferred_element_type=jnp.float32,
    ).T
    direct = lax.dot_general(
        incident[...],
        bem[...],
        (((1,), (1,)), ((), ())),
        precision=lax.Precision.HIGHEST,
        preferred_element_type=jnp.float32,
    )
    out[...] = (
        direct + spread[0:S] + spread[S : 2 * S] + spread[2 * S : 3 * S] + spread[3 * S :]
    )


def surface_apply(index, values, incident, bem):
    whole = pl.BlockSpec(memory_space=pltpu.VMEM)
    square = pltpu.VMEM((LANES, LANES), jnp.float32)
    return pl.pallas_call(
        surface_kernel,
        in_specs=[pl.BlockSpec(memory_space=pltpu.SMEM), whole, whole, whole],
        out_specs=whole,
        out_shape=jax.ShapeDtypeStruct((S, bem.shape[0]), jnp.float32),
        scratch_shapes=[pltpu.VMEM((bem.shape[1], LANES), jnp.float32)] + [square] * 4,
        compiler_params=pltpu.CompilerParams(vmem_limit_bytes=VMEM_BYTES),
        name="surface",
    )(index, values, incident, bem)


def shards(
    field, incident, elem_mat, connect, halo_lists, bem_rows, send_node, send_count, block_slots
):
    halo = halo_lists.shape[2]
    blocks = send_node.shape[1]
    slot_cap = send_node.shape[2]
    picked = pick(
        jnp.concatenate([halo_lists[0].reshape(-1), send_node[0].reshape(-1)]), field
    )
    count = lax.axis_size("row") * lax.axis_size("col")
    forward = [(i, i + 1) for i in range(count - 1)]
    backward = [(target, source) for source, target in forward]
    axes = ("row", "col")
    low = lax.ppermute(picked[:, halo : 2 * halo], axes, forward)
    high = lax.ppermute(picked[:, :halo], axes, backward)
    traces = picked[:, 2 * halo :].reshape(S, blocks, slot_cap)
    live_slots = jnp.arange(slot_cap, dtype=jnp.int32)[None, :] < send_count[0][:, None]
    traces = jnp.where(live_slots[None], traces, jnp.zeros_like(traces))
    outgoing = jnp.transpose(traces, (1, 0, 2))
    copies = lax.axis_size("row")
    spread = jnp.broadcast_to(outgoing[None], (copies,) + outgoing.shape).reshape(
        (copies * blocks,) + outgoing.shape[1:]
    )
    arrived = lax.all_to_all(spread, axes, split_axis=0, concat_axis=0, tiled=True)

    index = jnp.transpose(connect.reshape(4, -1, LANES), (1, 0, 2)).reshape(-1)
    fem_out = element_apply(index, elem_mat, low, field, high)

    values = jnp.transpose(arrived, (1, 0, 2)).reshape(S, -1)
    slots = block_slots[0].reshape(-1)
    first = jnp.sum(jnp.where(slots[None] == 0, values, 0.0), axis=1, keepdims=True)
    column = jnp.arange(incident.shape[1], dtype=jnp.int32)[None]
    incident = incident + jnp.where(column == 0, first, 0.0)
    partial_rows = surface_apply(slots, values, incident, bem_rows)
    bem_out = lax.psum(partial_rows, "col")
    return (fem_out, bem_out)


def solution(mesh):
    return jax.shard_map(
        shards,
        mesh=mesh,
        in_specs=(
            P(None, ("row", "col")),
            P(None, "col"),
            P(None, None, ("row", "col")),
            P(None, ("row", "col")),
            P(("row", "col"), None, None),
            P("row", "col"),
            P(("row", "col"), None, None),
            P(("row", "col"), None),
            P("col", None, None),
        ),
        out_specs=(P(None, ("row", "col")), P(None, "row")),
        check_vma=False,
    )
```

```python
import functools

import jax
import jax.numpy as jnp
from jax import lax
from jax.experimental import pallas as pl
from jax.experimental.pallas import tpu as pltpu
from jax.sharding import PartitionSpec as P

S = 32
LANES = 128
GROUP = 4 * LANES
SETS = 2
UNROLL = 64
VMEM_BYTES = 60 * 2**20


def lane_iota():
    return lax.broadcasted_iota(jnp.int32, (1, LANES), 1)


def quarter(parts):
    lane = lane_iota()
    low = jnp.where(lane < S, parts[0], parts[1])
    high = jnp.where(lane < 3 * S, parts[2], parts[3])
    return jnp.where(lane < 2 * S, low, high)


def aligned(start, size=LANES):
    return pl.ds(pl.multiple_of(start, LANES), size)


def fill_table(table, first, source):
    def step(i, carry):
        block = source[:, aligned(i * LANES)]
        table[aligned(first + i * LANES), :] = jnp.concatenate([block] * 4, axis=0).T
        return carry

    lax.fori_loop(0, source.shape[1] // LANES, step, 0)


def gather_rows(table, index, base, rows):
    def step(j, carry):
        start = pl.multiple_of(j * UNROLL, UNROLL)
        for u in range(UNROLL):
            picked = [
                table[pl.ds(index[base + b * LANES + start + u], 1), :] for b in range(4)
            ]
            rows[pl.ds(start + u, 1), :] = quarter(picked)
        return carry

    lax.fori_loop(0, LANES // UNROLL, step, 0)


def pick_kernel(index, field, out, table, rows):
    fill_table(table, 0, field)

    def group(k, carry):
        gather_rows(table, index, k * GROUP, rows)
        turned = rows[...].T
        for b in range(4):
            out[:, aligned(k * GROUP + b * LANES)] = turned[S * b : S * b + S]
        return carry

    lax.fori_loop(0, out.shape[1] // GROUP, group, 0)


def pick(index, field):
    return pl.pallas_call(
        pick_kernel,
        in_specs=[
            pl.BlockSpec(memory_space=pltpu.SMEM),
            pl.BlockSpec(memory_space=pltpu.VMEM),
        ],
        out_specs=pl.BlockSpec(memory_space=pltpu.VMEM),
        out_shape=jax.ShapeDtypeStruct((S, index.shape[0]), jnp.float32),
        scratch_shapes=[
            pltpu.VMEM((field.shape[1], LANES), jnp.float32),
            pltpu.VMEM((LANES, LANES), jnp.float32),
        ],
        compiler_params=pltpu.CompilerParams(vmem_limit_bytes=VMEM_BYTES),
        name="pick",
    )(index, field)


def element_kernel(halo, index, mats, low, field, high, out, table, *scratch):
    rows, terms, sums = scratch[:2], scratch[2:4], scratch[4:]
    step = pl.program_id(0)
    nodes = field.shape[1]

    @pl.when(step == 0)
    def _():
        fill_table(table, 0, low)
        fill_table(table, halo, field)
        fill_table(table, halo + nodes, high)

        def clear(i, carry):
            for total in sums:
                total[aligned(i * LANES), :] = jnp.zeros((LANES, LANES), jnp.float32)
            return carry

        lax.fori_loop(0, table.shape[0] // LANES, clear, 0)

    count = mats.shape[2] // LANES

    def gather_one(base, into, e):
        picked = [table[pl.ds(index[base + b * LANES + e], 1), :] for b in range(4)]
        into[pl.ds(e, 1), :] = quarter(picked)

    def scatter_some(base, source, e):
        places, values = [], []
        for p in range(SETS):
            term = source[pl.ds(e + p, 1), :]
            for a in range(4):
                place = pl.ds(index[base + a * LANES + e + p], 1)
                places.append(place)
                values.append(sums[4 * p + a][place, :] + term)
        for total, place, value in zip(sums, places, values):
            total[place, :] = value

    def multiply(k, source, into):
        turned = source[...].T
        here = aligned(k * LANES)
        parts = []
        for a in range(4):
            part = mats[a, 0:1, here] * turned[0:S]
            for b in range(1, 4):
                part = part + mats[a, b : b + 1, here] * turned[S * b : S * b + S]
            parts.append(part)
        into[...] = jnp.concatenate(parts, axis=0).T

    gather_rows(table, index, 0, rows[0])
    terms[1][...] = jnp.zeros((LANES, LANES), jnp.float32)

    def pair(i, carry):
        for half in range(2):
            k = 2 * i + half
            ahead = jnp.minimum(k + 1, count - 1) * GROUP
            behind = jnp.maximum(k - 1, 0) * GROUP
            multiply(k, rows[half], terms[half])
            for e in range(0, LANES, SETS):
                for p in range(SETS):
                    gather_one(ahead, rows[1 - half], e + p)
                scatter_some(behind, terms[1 - half], e)
        return carry

    lax.fori_loop(0, count // 2, pair, 0)

    def drain(j, carry):
        start = pl.multiple_of(j * UNROLL, UNROLL)
        for u in range(0, UNROLL, SETS):
            scatter_some((count - 1) * GROUP, terms[1], start + u)
        return carry

    lax.fori_loop(0, LANES // UNROLL, drain, 0)

    @pl.when(step == pl.num_programs(0) - 1)
    def _():
        def finish(i, carry):
            here = aligned(i * LANES + halo)
            added = [
                sum(sums[4 * p + a][here, :] for p in range(1, SETS)) + sums[a][here, :]
                for a in range(4)
            ]
            turned = quarter(added).T
            out[:, aligned(i * LANES)] = (
                turned[0:S] + turned[S : 2 * S] + turned[2 * S : 3 * S] + turned[3 * S :]
            )
            return carry

        lax.fori_loop(0, nodes // LANES, finish, 0)


def element_apply(index, mats, low, field, high):
    halo, nodes = low.shape[1], field.shape[1]
    elements = mats.shape[2]
    blocks = next(n for n in (48, 32, 24, 16, 12, 8, 4, 2) if elements % (n * LANES) == 0)
    table = pltpu.VMEM((nodes + 2 * halo, LANES), jnp.float32)
    square = pltpu.VMEM((LANES, LANES), jnp.float32)
    whole = pl.BlockSpec(memory_space=pltpu.VMEM)
    return pl.pallas_call(
        functools.partial(element_kernel, halo),
        grid=(elements // (blocks * LANES),),
        in_specs=[
            pl.BlockSpec((blocks * GROUP,), lambda i: (i,), memory_space=pltpu.SMEM),
            pl.BlockSpec((4, 4, blocks * LANES), lambda i: (0, 0, i)),
            whole,
            whole,
            whole,
        ],
        out_specs=whole,
        out_shape=jax.ShapeDtypeStruct((S, nodes), jnp.float32),
        scratch_shapes=[table] + [square] * 4 + [table] * (4 * SETS),
        compiler_params=pltpu.CompilerParams(vmem_limit_bytes=VMEM_BYTES),
        name="elements",
    )(index, mats, low, field, high)


def surface_kernel(index, values, incident, bem, out, surface, *rows):
    lane = lane_iota()

    def group(k, carry):
        stacked = jnp.concatenate(
            [values[:, aligned(k * GROUP + q * LANES)] for q in range(4)], axis=0
        )
        turned = stacked.T
        for q in range(4):
            rows[q][...] = jnp.where(
                (lane >= S * q) & (lane < S * q + S), turned, jnp.zeros_like(turned)
            )

        def scatter(j, inner):
            start = pl.multiple_of(j * UNROLL, UNROLL)
            for u in range(UNROLL):
                for q in range(4):
                    place = index[k * GROUP + q * LANES + start + u]
                    surface[pl.ds(place, 1), :] = rows[q][pl.ds(start + u, 1), :]
            return inner

        lax.fori_loop(0, LANES // UNROLL, scatter, 0)
        return carry

    lax.fori_loop(0, values.shape[1] // GROUP, group, 0)
    surface[0:1, :] = jnp.zeros((1, LANES), jnp.float32)
    spread = jnp.dot(
        bem[...],
        surface[...],
        precision=lax.Precision.HIGHEST,
        preferred_element_type=jnp.float32,
    ).T
    direct = lax.dot_general(
        incident[...],
        bem[...],
        (((1,), (1,)), ((), ())),
        precision=lax.Precision.HIGHEST,
        preferred_element_type=jnp.float32,
    )
    out[...] = (
        direct + spread[0:S] + spread[S : 2 * S] + spread[2 * S : 3 * S] + spread[3 * S :]
    )


def surface_apply(index, values, incident, bem):
    whole = pl.BlockSpec(memory_space=pltpu.VMEM)
    square = pltpu.VMEM((LANES, LANES), jnp.float32)
    return pl.pallas_call(
        surface_kernel,
        in_specs=[pl.BlockSpec(memory_space=pltpu.SMEM), whole, whole, whole],
        out_specs=whole,
        out_shape=jax.ShapeDtypeStruct((S, bem.shape[0]), jnp.float32),
        scratch_shapes=[pltpu.VMEM((bem.shape[1], LANES), jnp.float32)] + [square] * 4,
        compiler_params=pltpu.CompilerParams(vmem_limit_bytes=VMEM_BYTES),
        name="surface",
    )(index, values, incident, bem)


def shards(
    field, incident, elem_mat, connect, halo_lists, bem_rows, send_node, send_count, block_slots
):
    halo = halo_lists.shape[2]
    blocks = send_node.shape[1]
    slot_cap = send_node.shape[2]
    picked = pick(
        jnp.concatenate([halo_lists[0].reshape(-1), send_node[0].reshape(-1)]), field
    )
    count = lax.axis_size("row") * lax.axis_size("col")
    forward = [(i, i + 1) for i in range(count - 1)]
    backward = [(target, source) for source, target in forward]
    axes = ("row", "col")
    low = lax.ppermute(picked[:, halo : 2 * halo], axes, forward)
    high = lax.ppermute(picked[:, :halo], axes, backward)
    traces = picked[:, 2 * halo :].reshape(S, blocks, slot_cap)
    live_slots = jnp.arange(slot_cap, dtype=jnp.int32)[None, :] < send_count[0][:, None]
    traces = jnp.where(live_slots[None], traces, jnp.zeros_like(traces))
    outgoing = jnp.transpose(traces, (1, 0, 2))
    copies = lax.axis_size("row")
    spread = jnp.broadcast_to(outgoing[None], (copies,) + outgoing.shape).reshape(
        (copies * blocks,) + outgoing.shape[1:]
    )
    arrived = lax.all_to_all(spread, axes, split_axis=0, concat_axis=0, tiled=True)

    index = jnp.transpose(connect.reshape(4, -1, LANES), (1, 0, 2)).reshape(-1)
    fem_out = element_apply(index, elem_mat, low, field, high)

    values = jnp.transpose(arrived, (1, 0, 2)).reshape(S, -1)
    slots = block_slots[0].reshape(-1)
    first = jnp.sum(jnp.where(slots[None] == 0, values, 0.0), axis=1, keepdims=True)
    column = jnp.arange(incident.shape[1], dtype=jnp.int32)[None]
    incident = incident + jnp.where(column == 0, first, 0.0)
    partial_rows = surface_apply(slots, values, incident, bem_rows)
    bem_out = lax.psum(partial_rows, "col")
    return (fem_out, bem_out)


def solution(mesh):
    return jax.shard_map(
        shards,
        mesh=mesh,
        in_specs=(
            P(None, ("row", "col")),
            P(None, "col"),
            P(None, None, ("row", "col")),
            P(None, ("row", "col")),
            P(("row", "col"), None, None),
            P("row", "col"),
            P(("row", "col"), None, None),
            P(("row", "col"), None),
            P("col", None, None),
        ),
        out_specs=(P(None, ("row", "col")), P(None, "row")),
        check_vma=False,
    )
```
